32 devices in a mesh: band: 4 (over y, core), col: 8 (over z, x).
Axes of the slice: x: 2, y: 2, z: 4, core: 2. Of those that a mesh axis runs over, the one named last changes fastest.
Arguments:
- intersections: bfloat16 [8, 1024, 512], P('band'), may hold values from -6 to 6
- screened: bfloat16 [1024, 1024], P('band', 'col'), may hold values from -0.1875 to 0.1875
- poles: bfloat16 [1024, 1024], P('band', 'col'), may hold values from 0.5 to 4
- gap_energy: float32 [3], replicated, may hold values from 0.3 to 3
- gap_class: int32 [8, 512], P('band'), may hold values from 0 to 2
Outputs:
- sigma: float32 [512, 512], P('band', 'col')
The draws below stay inside these ranges and needn't reach their ends.
All inputs are finite; a program needn't handle non-finite values.
Results may differ from the reference program's by a relative error of at most 0.0041.
Values may be sent and summed in bfloat16 or wider, within the bound.
A program may use at most 64 MiB of HBM per device.

```python
import math
import jax
import jax.numpy as jnp
from jax import lax

S = 512
CLASSES = 3
NG = 1024
NB = 8


def touch_ends(entries, rng, least, high):
    dims = entries.shape
    place = [jax.random.randint(jax.random.fold_in(rng, axis), (), 0, dims[axis]) for axis in range(len(dims))]
    entries = entries.at[tuple(place)].set(least)
    longest = dims.index(max(dims))
    place[longest] = (place[longest] + 1) % dims[longest]
    return entries.at[tuple(place)].set(high)


def block_scale(own_key, extent, split, smallest, high):
    loudness = 1.0
    for dim, shards_of in split:
        steps = jax.random.uniform(jax.random.fold_in(jax.random.fold_in(own_key, 6), dim), (shards_of,), jnp.float32, smallest / len(split), high / len(split))
        loudness = loudness * jnp.repeat(jnp.exp(steps), extent[dim] // shards_of).reshape((-1,) + (1,) * (len(extent) - 1 - dim))
    return loudness


def scatter_about(key, dims, deviation, limit, shards=(), kind=jnp.bfloat16):
    array = deviation * jax.random.normal(key, dims, jnp.float32)
    if shards:
        array = array * block_scale(key, dims, shards, -0.22, 0.18)
    return jnp.clip(array, -limit, limit).astype(kind)


def setup_inputs(seed: int = 0) -> dict:
    key_of = jax.random.split(jax.random.key(seed), 6)
    intersections = scatter_about(key_of[0], (NB, NG, S), 1.0, 6.0, ((0, 4),))
    screened = scatter_about(key_of[1], (NG, NG), NG ** -0.5, 0.1875, ((0, 4), (1, 8)))
    poles = jnp.clip(jnp.exp(math.log(4.0) - 2.0794415 * jax.random.uniform(key_of[2], (NG, NG), jnp.float32) ** block_scale(key_of[2], (NG, NG), ((0, 4), (1, 8)), -0.2, 0.2)), 0.5, 4.0).astype(jnp.bfloat16)
    gap_energy = jnp.clip(jnp.exp(jax.random.uniform(key_of[3], (CLASSES,), jnp.float32, math.log(0.3), math.log(3.0))), 0.3, 3.0)
    gap_class = touch_ends(jax.random.randint(key_of[4], (NB, S), 0, CLASSES), jax.random.fold_in(key_of[4], 1), 0, CLASSES - 1).astype(jnp.int32)
    return dict(intersections=intersections, screened=screened, poles=poles, gap_energy=gap_energy, gap_class=gap_class)


def reference(intersections, screened, poles, gap_energy, gap_class):
    amps = screened.astype(jnp.float32)
    freqs = poles.astype(jnp.float32)
    factors = []
    for class_id in range(CLASSES):
        energy = gap_energy[class_id]
        value = amps * freqs / (freqs * freqs + energy * energy)
        factors.append(value.astype(jnp.bfloat16).astype(jnp.float32))

    def one_band(carry, inputs):
        band_rows, band_class = inputs
        left = band_rows.astype(jnp.float32)
        side = jnp.zeros((S, NG), jnp.float32)
        for class_id in range(CLASSES):
            term = lax.dot_general(left, factors[class_id], (((0,), (0,)), ((), ())), precision=lax.Precision.HIGHEST, preferred_element_type=jnp.float32)
            picked = (band_class == class_id).astype(jnp.float32)
            side = side + picked[:, None] * term
        rounded = side.astype(jnp.bfloat16).astype(jnp.float32)
        return (carry + jnp.dot(rounded, left, precision=lax.Precision.HIGHEST, preferred_element_type=jnp.float32), None)
    total, _ = lax.scan(one_band, jnp.zeros((S, S), jnp.float32), (intersections, gap_class))
    return total / jnp.sqrt(jnp.float32(NG * NB))
```

```python
import functools
import math

import jax
import jax.numpy as jnp
from jax import lax
from jax.experimental import pallas as pl
from jax.experimental.pallas import tpu as pltpu
from jax.sharding import PartitionSpec as P

MESH = pl.DeviceIdType.MESH


def flip(pos, mask):
    bit = 1
    while bit <= mask:
        if mask & bit:
            pos = pos + bit - 2 * bit * lax.rem(lax.div(pos, bit), 2)
        bit *= 2
    return pos


def kernel(
    nband, ncol, classes, scale,
    inter_ref, screened_ref, poles_ref, energy_ref, class_ref, out_ref,
    inter, held, energies, cls, side, side_parts, right_all, right, own,
    core_out, core_in, band_out, band_in, col_out, col_in,
    load_sem, gather_send, gather_recv, core_send, core_recv,
    band_send, band_recv, col_send, col_recv,
):
    me, col = lax.axis_index("band"), lax.axis_index("col")
    bands, _, states = inter.shape
    depth, columns = screened_ref.shape
    half = nband // 2
    width = states // nband
    rows = states // ncol

    barrier = pltpu.get_barrier_semaphore()
    peers = [(flip(me, mask), col) for mask in [1] + list(range(2, nband, 2))]
    peers += [(me, flip(col, piece)) for piece in range(1, ncol)]
    for peer in peers:
        pl.semaphore_signal(barrier, inc=1, device_id=peer, device_id_type=MESH)

    loads = [
        pltpu.make_async_copy(screened_ref, held.at[0, 0], load_sem.at[0]),
        pltpu.make_async_copy(poles_ref, held.at[0, 1], load_sem.at[1]),
        pltpu.make_async_copy(energy_ref, energies, load_sem.at[2]),
        pltpu.make_async_copy(class_ref, cls, load_sem.at[3]),
        pltpu.make_async_copy(inter_ref, inter, load_sem.at[4]),
    ]
    for load in loads:
        load.start()
    pl.semaphore_wait(barrier, len(peers))

    arriving = {}

    def push(slot, bit, part):
        source = (screened_ref, poles_ref)[part] if slot == 0 else held.at[slot, part]
        copy = pltpu.make_async_remote_copy(
            src_ref=source,
            dst_ref=held.at[slot + bit, part],
            send_sem=gather_send.at[slot + bit, part],
            recv_sem=gather_recv.at[slot + bit, part],
            device_id=(flip(me, bit), col),
            device_id_type=MESH,
        )
        copy.start()
        arriving[slot + bit, part] = copy

    bit = half
    while bit:
        push(0, bit, 0)
        push(0, bit, 1)
        bit //= 2
    for load in loads:
        load.wait()

    def add_block(slot):
        amps = held[slot, 0].astype(jnp.float32).T
        freqs = held[slot, 1].astype(jnp.float32).T
        top, square = amps * freqs, freqs * freqs
        factors = []
        for class_id in range(classes):
            energy = energies[class_id]
            factors.append((top / (square + energy * energy)).astype(jnp.bfloat16))
        factors = jnp.concatenate(factors, axis=0)
        start = pl.multiple_of(flip(me, slot) * depth, depth)
        for band in range(bands):
            terms = jnp.dot(
                factors, inter[band, pl.ds(start, depth), :], preferred_element_type=jnp.float32
            )
            picked = jnp.zeros((columns, states), jnp.float32)
            for class_id in range(classes):
                term = terms[class_id * columns:(class_id + 1) * columns]
                picked = jnp.where(cls[band:band + 1, :] == class_id, term, picked)
            place = slice(band * columns, (band + 1) * columns)
            side[place, :] = picked if slot == 0 else side[place, :] + picked

    add_block(0)
    first = pl.multiple_of(col * columns, columns)
    for band in range(bands):
        block = inter[band, pl.ds(first, columns), :].astype(jnp.float32)
        right_all[:, band * columns:(band + 1) * columns] = block.T.astype(jnp.bfloat16)
    for piece in range(ncol):
        start = pl.multiple_of(flip(col, piece) * rows, rows)
        right[piece * rows:(piece + 1) * rows, :] = right_all[pl.ds(start, rows), :]

    for slot in range(1, nband):
        for part in range(2):
            arriving[slot, part].wait_recv()
            bit = (slot & -slot) // 2
            while bit:
                push(slot, bit, part)
                bit //= 2
        add_block(slot)
    for block in range(nband):
        part = side[:, block * width:(block + 1) * width]
        side_parts[block] = part.astype(jnp.bfloat16)

    order = list(range(ncol - 1, -1, -1))

    def sides_of(base):
        return jnp.concatenate(
            [side_parts[flip(base, 2 * k)] for k in range(half)], axis=1
        )

    other = sides_of(flip(me, 1))
    core = {}
    group = max(1, ncol // 2)
    for low in range(ncol - group, -1, -group):
        product = jnp.dot(
            right[low * rows:(low + group) * rows, :], other, preferred_element_type=jnp.float32
        ).astype(jnp.bfloat16)
        for piece in range(low + group - 1, low - 1, -1):
            at = (piece - low) * rows
            for k in range(half):
                core_out[piece, k] = product[at:at + rows, k * width:(k + 1) * width]
            core[piece] = pltpu.make_async_remote_copy(
                src_ref=core_out.at[piece],
                dst_ref=core_in.at[piece],
                send_sem=core_send.at[piece],
                recv_sem=core_recv.at[piece],
                device_id=(flip(me, 1), col),
                device_id_type=MESH,
            )
            core[piece].start()
    own[...] = jnp.dot(right[...], sides_of(me), preferred_element_type=jnp.float32)

    across = {}
    for piece in order:
        core[piece].wait_recv()
        at = slice(piece * rows, (piece + 1) * rows)
        for k in range(half - 1, -1, -1):
            lanes = slice(k * width, (k + 1) * width)
            value = own[at, lanes] + core_in[piece, k].astype(jnp.float32)
            if k == 0:
                own[at, lanes] = value
                continue
            band_out[piece, k] = value.astype(jnp.bfloat16)
            across[piece, k] = pltpu.make_async_remote_copy(
                src_ref=band_out.at[piece, k],
                dst_ref=band_in.at[piece, k],
                send_sem=band_send.at[piece, k],
                recv_sem=band_recv.at[piece, k],
                device_id=(flip(me, 2 * k), col),
                device_id_type=MESH,
            )
            across[piece, k].start()

    last = {}
    for piece in order:
        value = own[piece * rows:(piece + 1) * rows, 0:width]
        for k in range(1, half):
            across[piece, k].wait_recv()
            value = value + band_in[piece, k].astype(jnp.float32)
        if piece == 0:
            break
        col_out[piece] = value.astype(jnp.bfloat16)
        last[piece] = pltpu.make_async_remote_copy(
            src_ref=col_out.at[piece],
            dst_ref=col_in.at[piece],
            send_sem=col_send.at[piece],
            recv_sem=col_recv.at[piece],
            device_id=(me, flip(col, piece)),
            device_id_type=MESH,
        )
        last[piece].start()
    for piece in range(1, ncol):
        last[piece].wait_recv()
        value = value + col_in[piece].astype(jnp.float32)
    out_ref[...] = value * scale

    for group_of in (arriving, core, across, last):
        for copy in group_of.values():
            copy.wait_send()


def local(nband, ncol, intersections, screened, poles, gap_energy, gap_class):
    bands, g_rows, states = intersections.shape
    depth, columns = screened.shape
    classes = gap_energy.shape[0]
    half, width, rows = nband // 2, states // nband, states // ncol
    scale = 1.0 / math.sqrt(columns * ncol * bands * nband)
    bf16, f32 = jnp.bfloat16, jnp.float32
    dma = pltpu.SemaphoreType.DMA
    block = pl.pallas_call(
        functools.partial(kernel, nband, ncol, classes, scale),
        out_shape=jax.ShapeDtypeStruct((rows, width), f32),
        in_specs=[pl.BlockSpec(memory_space=pl.ANY)] * 5,
        out_specs=pl.BlockSpec(memory_space=pltpu.VMEM),
        scratch_shapes=[
            pltpu.VMEM((bands, g_rows, states), bf16),
            pltpu.VMEM((nband, 2, depth, columns), bf16),
            pltpu.SMEM((classes,), f32),
            pltpu.VMEM((bands, states), jnp.int32),
            pltpu.VMEM((bands * columns, states), f32),
            pltpu.VMEM((nband, bands * columns, width), bf16),
            pltpu.VMEM((states, bands * columns), bf16),
            pltpu.VMEM((states, bands * columns), bf16),
            pltpu.VMEM((states, half * width), f32),
            pltpu.VMEM((ncol, half, rows, width), bf16),
            pltpu.VMEM((ncol, half, rows, width), bf16),
            pltpu.VMEM((ncol, half, rows, width), bf16),
            pltpu.VMEM((ncol, half, rows, width), bf16),
            pltpu.VMEM((ncol, rows, width), bf16),
            pltpu.VMEM((ncol, rows, width), bf16),
            dma((5,)),
            dma((nband, 2)), dma((nband, 2)),
            dma((ncol,)), dma((ncol,)),
            dma((ncol, half)), dma((ncol, half)),
            dma((ncol,)), dma((ncol,)),
        ],
        compiler_params=pltpu.CompilerParams(
            collective_id=0, has_side_effects=True, vmem_limit_bytes=56 * 1024 * 1024
        ),
        name="self_energy",
    )(intersections, screened, poles, gap_energy, gap_class)
    return block.T


def solution(mesh):
    return jax.shard_map(
        functools.partial(local, mesh.shape["band"], mesh.shape["col"]),
        mesh=mesh,
        in_specs=(P("band", None, None), P("band", "col"), P("band", "col"), P(), P("band", None)),
        out_specs=P("band", "col"),
        check_vma=False,
    )
```

```python
import functools
import math

import jax
import jax.numpy as jnp
from jax import lax
from jax.experimental import pallas as pl
from jax.experimental.pallas import tpu as pltpu
from jax.sharding import PartitionSpec as P

MESH = pl.DeviceIdType.MESH


def flip(pos, mask):
    bit = 1
    while bit <= mask:
        if mask & bit:
            pos = pos + bit - 2 * bit * lax.rem(lax.div(pos, bit), 2)
        bit *= 2
    return pos


def kernel(
    nband, ncol, classes, scale, aligned,
    inter_ref, screened_ref, poles_ref, energy_ref, class_ref, out_ref,
    inter, held, energies, cls, cross, side, side_parts, right_all, right, own,
    band_out, band_in, col_out, col_in,
    load_sem, gather_send, gather_recv, swap_send, swap_recv,
    band_send, band_recv, col_send, col_recv,
):
    me, col = lax.axis_index("band"), lax.axis_index("col")
    bands, _, states = inter_ref.shape
    depth, columns = screened_ref.shape
    half = nband // 2
    width = states // nband
    rows = states // ncol
    sibling = flip(me, 1)
    first = pl.multiple_of(col * columns, columns)

    barrier = pltpu.get_barrier_semaphore()
    peers = [(flip(me, mask), col) for mask in [1] + list(range(2, nband, 2))]
    peers += [(me, flip(col, piece)) for piece in range(1, ncol)]
    for peer in peers:
        pl.semaphore_signal(barrier, inc=1, device_id=peer, device_id_type=MESH)

    def shares(owner, slot):
        out = [(inter_ref.at[:, pl.ds(first, columns), :], cross.at[slot])]
        if not aligned:
            out += [(class_ref, cls.at[slot]), (inter_ref, inter.at[slot])]
            return out
        for k in range(half):
            start = pl.multiple_of(flip(owner, 2 * k) * width, width)
            lanes = slice(k * width, (k + 1) * width)
            out.append((class_ref.at[:, pl.ds(start, width)], cls.at[slot, :, lanes]))
            out.append((inter_ref.at[:, :, pl.ds(start, width)], inter.at[slot, :, :, lanes]))
        return out

    pairs = [
        (screened_ref, held.at[0, 0]), (poles_ref, held.at[0, 1]), (energy_ref, energies),
    ] + shares(me, 0)
    loads = [
        pltpu.make_async_copy(source, target, load_sem.at[n])
        for n, (source, target) in enumerate(pairs)
    ]
    for load in loads:
        load.start()
    pl.semaphore_wait(barrier, len(peers))

    arriving = {}

    def push(slot, bit, part):
        source = (screened_ref, poles_ref)[part] if slot == 0 else held.at[slot, part]
        copy = pltpu.make_async_remote_copy(
            src_ref=source,
            dst_ref=held.at[slot + bit, part],
            send_sem=gather_send.at[slot + bit, part],
            recv_sem=gather_recv.at[slot + bit, part],
            device_id=(flip(me, bit), col),
            device_id_type=MESH,
        )
        copy.start()
        arriving[slot + bit, part] = copy

    bit = half
    while bit:
        push(0, bit, 0)
        push(0, bit, 1)
        bit //= 2
    swap = {}
    for n, (source, target) in enumerate(shares(sibling, 1)):
        swap[n] = pltpu.make_async_remote_copy(
            src_ref=source,
            dst_ref=target,
            send_sem=swap_send.at[n],
            recv_sem=swap_recv.at[n],
            device_id=(sibling, col),
            device_id_type=MESH,
        )
        swap[n].start()
    for load in loads:
        load.wait()

    def add_block(slot):
        amps = held[slot, 0].astype(jnp.float32).T
        freqs = held[slot, 1].astype(jnp.float32).T
        top, square = amps * freqs, freqs * freqs
        factors = []
        for class_id in range(classes):
            energy = energies[class_id]
            factors.append((top / (square + energy * energy)).astype(jnp.bfloat16))
        factors = jnp.concatenate(factors, axis=0)
        start = pl.multiple_of(flip(me, slot) * depth, depth)
        for band in range(2 * bands):
            core, index = divmod(band, bands)
            terms = jnp.dot(
                factors, inter[core, index, pl.ds(start, depth), :],
                preferred_element_type=jnp.float32,
            )
            picked = jnp.zeros((columns, terms.shape[1]), jnp.float32)
            for class_id in range(classes):
                term = terms[class_id * columns:(class_id + 1) * columns]
                picked = jnp.where(cls[core, index:index + 1, :] == class_id, term, picked)
            place = slice(band * columns, (band + 1) * columns)
            side[place, :] = picked if slot == 0 else side[place, :] + picked

    def turn(core):
        for band in range(bands):
            block = cross[core, band].astype(jnp.float32)
            low = (core * bands + band) * columns
            right_all[:, low:low + columns] = block.T.astype(jnp.bfloat16)

    turn(0)
    for copy in swap.values():
        copy.wait_recv()
    add_block(0)
    turn(1)
    for piece in range(ncol):
        start = pl.multiple_of(flip(col, piece) * rows, rows)
        right[piece * rows:(piece + 1) * rows, :] = right_all[pl.ds(start, rows), :]

    for slot in range(1, nband):
        for part in range(2):
            arriving[slot, part].wait_recv()
            bit = (slot & -slot) // 2
            while bit:
                push(slot, bit, part)
                bit //= 2
        add_block(slot)
    if aligned:
        sides = side[...].astype(jnp.bfloat16)
    else:
        for block in range(nband):
            part = side[:, block * width:(block + 1) * width]
            side_parts[block] = part.astype(jnp.bfloat16)
        sides = jnp.concatenate([side_parts[flip(me, 2 * k)] for k in range(half)], axis=1)

    across = {}
    group = max(1, ncol // 2)
    for low in range(ncol - group, -1, -group):
        product = jnp.dot(
            right[low * rows:(low + group) * rows, :], sides, preferred_element_type=jnp.float32
        )
        own[low * rows:(low + group) * rows, :] = product[:, 0:width]
        for piece in range(low + group - 1, low - 1, -1):
            at = slice((piece - low) * rows, (piece - low + 1) * rows)
            for k in range(half - 1, 0, -1):
                band_out[piece, k] = product[at, k * width:(k + 1) * width].astype(jnp.bfloat16)
                across[piece, k] = pltpu.make_async_remote_copy(
                    src_ref=band_out.at[piece, k],
                    dst_ref=band_in.at[piece, k],
                    send_sem=band_send.at[piece, k],
                    recv_sem=band_recv.at[piece, k],
                    device_id=(flip(me, 2 * k), col),
                    device_id_type=MESH,
                )
                across[piece, k].start()

    last = {}
    for piece in range(ncol - 1, -1, -1):
        value = own[piece * rows:(piece + 1) * rows, :]
        for k in range(1, half):
            across[piece, k].wait_recv()
            value = value + band_in[piece, k].astype(jnp.float32)
        if piece == 0:
            break
        col_out[piece] = value.astype(jnp.bfloat16)
        last[piece] = pltpu.make_async_remote_copy(
            src_ref=col_out.at[piece],
            dst_ref=col_in.at[piece],
            send_sem=col_send.at[piece],
            recv_sem=col_recv.at[piece],
            device_id=(me, flip(col, piece)),
            device_id_type=MESH,
        )
        last[piece].start()
    for piece in range(1, ncol):
        last[piece].wait_recv()
        value = value + col_in[piece].astype(jnp.float32)
    out_ref[...] = value * scale

    for group_of in (arriving, swap, across, last):
        for copy in group_of.values():
            copy.wait_send()


def local(nband, ncol, intersections, screened, poles, gap_energy, gap_class):
    bands, g_rows, states = intersections.shape
    depth, columns = screened.shape
    classes = gap_energy.shape[0]
    half, width, rows = nband // 2, states // nband, states // ncol
    scale = 1.0 / math.sqrt(columns * ncol * bands * nband)
    bf16, f32 = jnp.bfloat16, jnp.float32
    dma = pltpu.SemaphoreType.DMA
    aligned = width % 128 == 0
    lanes = half * width if aligned else states
    shares = 1 + 2 * (half if aligned else 1)
    block = pl.pallas_call(
        functools.partial(kernel, nband, ncol, classes, scale, aligned),
        out_shape=jax.ShapeDtypeStruct((rows, width), f32),
        in_specs=[pl.BlockSpec(memory_space=pl.ANY)] * 5,
        out_specs=pl.BlockSpec(memory_space=pltpu.VMEM),
        scratch_shapes=[
            pltpu.VMEM((2, bands, g_rows, lanes), bf16),
            pltpu.VMEM((nband, 2, depth, columns), bf16),
            pltpu.SMEM((classes,), f32),
            pltpu.VMEM((2, bands, lanes), jnp.int32),
            pltpu.VMEM((2, bands, columns, states), bf16),
            pltpu.VMEM((2 * bands * columns, lanes), f32),
            pltpu.VMEM((1 if aligned else nband, 2 * bands * columns, width), bf16),
            pltpu.VMEM((states, 2 * bands * columns), bf16),
            pltpu.VMEM((states, 2 * bands * columns), bf16),
            pltpu.VMEM((states, width), f32),
            pltpu.VMEM((ncol, half, rows, width), bf16),
            pltpu.VMEM((ncol, half, rows, width), bf16),
            pltpu.VMEM((ncol, rows, width), bf16),
            pltpu.VMEM((ncol, rows, width), bf16),
            dma((3 + shares,)),
            dma((nband, 2)), dma((nband, 2)),
            dma((shares,)), dma((shares,)),
            dma((ncol, half)), dma((ncol, half)),
            dma((ncol,)), dma((ncol,)),
        ],
        compiler_params=pltpu.CompilerParams(
            collective_id=0, has_side_effects=True, vmem_limit_bytes=56 * 1024 * 1024
        ),
        name="self_energy",
    )(intersections, screened, poles, gap_energy, gap_class)
    return block.T


def solution(mesh):
    return jax.shard_map(
        functools.partial(local, mesh.shape["band"], mesh.shape["col"]),
        mesh=mesh,
        in_specs=(P("band", None, None), P("band", "col"), P("band", "col"), P(), P("band", None)),
        out_specs=P("band", "col"),
        check_vma=False,
    )
```

```python
import functools
import math

import jax
import jax.numpy as jnp
from jax import lax
from jax.experimental import pallas as pl
from jax.experimental.pallas import tpu as pltpu
from jax.sharding import PartitionSpec as P

MESH = pl.DeviceIdType.MESH


def flip(pos, mask):
    bit = 1
    while bit <= mask:
        if mask & bit:
            pos = pos + bit - 2 * bit * lax.rem(lax.div(pos, bit), 2)
        bit *= 2
    return pos


def kernel(
    nband, ncol, classes, scale, aligned,
    inter_ref, screened_ref, poles_ref, energy_ref, class_ref, out_ref,
    inter, held, energies, cls, cross, factors, side, side_parts, right_all, right, own,
    band_out, band_in, col_out, col_in,
    load_sem, gather_send, gather_recv, swap_send, swap_recv,
    band_send, band_recv, col_send, col_recv,
):
    me, col = lax.axis_index("band"), lax.axis_index("col")
    bands, _, states = inter_ref.shape
    depth, columns = screened_ref.shape
    half = nband // 2
    width = states // nband
    rows = states // ncol
    sibling = flip(me, 1)
    first = pl.multiple_of(col * columns, columns)

    barrier = pltpu.get_barrier_semaphore()
    peers = [(flip(me, mask), col) for mask in [1] + list(range(2, nband, 2))]
    peers += [(me, flip(col, piece)) for piece in range(1, ncol)]
    for peer in peers:
        pl.semaphore_signal(barrier, inc=1, device_id=peer, device_id_type=MESH)

    def shares(owner, slot):
        out = [(inter_ref.at[:, pl.ds(first, columns), :], cross.at[slot])]
        if not aligned:
            out += [(class_ref, cls.at[slot]), (inter_ref, inter.at[slot])]
            return out
        for k in range(half):
            start = pl.multiple_of(flip(owner, 2 * k) * width, width)
            lanes = slice(k * width, (k + 1) * width)
            out.append((class_ref.at[:, pl.ds(start, width)], cls.at[slot, :, lanes]))
            out.append((inter_ref.at[:, :, pl.ds(start, width)], inter.at[slot, :, :, lanes]))
        return out

    pairs = [
        (screened_ref, held.at[0, 0]), (poles_ref, held.at[0, 1]), (energy_ref, energies),
    ] + shares(me, 0)
    loads = [
        pltpu.make_async_copy(source, target, load_sem.at[n])
        for n, (source, target) in enumerate(pairs)
    ]
    for load in loads:
        load.start()
    pl.semaphore_wait(barrier, len(peers))

    arriving = {}

    def push(slot, bit, part):
        source = (screened_ref, poles_ref)[part] if slot == 0 else held.at[slot, part]
        copy = pltpu.make_async_remote_copy(
            src_ref=source,
            dst_ref=held.at[slot + bit, part],
            send_sem=gather_send.at[slot + bit, part],
            recv_sem=gather_recv.at[slot + bit, part],
            device_id=(flip(me, bit), col),
            device_id_type=MESH,
        )
        copy.start()
        arriving[slot + bit, part] = copy

    bit = half
    while bit:
        push(0, bit, 0)
        push(0, bit, 1)
        bit //= 2
    swap = {}
    for n, (source, target) in enumerate(shares(sibling, 1)):
        swap[n] = pltpu.make_async_remote_copy(
            src_ref=source,
            dst_ref=target,
            send_sem=swap_send.at[n],
            recv_sem=swap_recv.at[n],
            device_id=(sibling, col),
            device_id_type=MESH,
        )
        swap[n].start()
    for load in loads:
        load.wait()

    def make_factors(slot):
        amps = held[slot, 0].astype(jnp.float32).T
        freqs = held[slot, 1].astype(jnp.float32).T
        top, square = amps * freqs, freqs * freqs
        for class_id in range(classes):
            energy = energies[class_id]
            factor = (top / (square + energy * energy)).astype(jnp.bfloat16)
            factors[slot, class_id * columns:(class_id + 1) * columns, :] = factor

    def add_block(slot, core):
        start = pl.multiple_of(flip(me, slot) * depth, depth)
        for index in range(bands):
            terms = jnp.dot(
                factors[slot], inter[core, index, pl.ds(start, depth), :],
                preferred_element_type=jnp.float32,
            )
            picked = jnp.zeros((columns, terms.shape[1]), jnp.float32)
            for class_id in range(classes):
                term = terms[class_id * columns:(class_id + 1) * columns]
                picked = jnp.where(cls[core, index:index + 1, :] == class_id, term, picked)
            low = (core * bands + index) * columns
            place = slice(low, low + columns)
            side[place, :] = picked if slot == 0 else side[place, :] + picked

    def turn(core):
        for band in range(bands):
            block = cross[core, band].astype(jnp.float32)
            low = (core * bands + band) * columns
            right_all[:, low:low + columns] = block.T.astype(jnp.bfloat16)

    make_factors(0)
    add_block(0, 0)
    turn(0)

    def pass_on(slot, part):
        arriving[slot, part].wait_recv()
        bit = (slot & -slot) // 2
        while bit:
            push(slot, bit, part)
            bit //= 2

    for slot in range(1, nband):
        pass_on(slot, 0)
        if slot == half:
            for copy in swap.values():
                copy.wait_recv()
            turn(1)
            for piece in range(ncol):
                start = pl.multiple_of(flip(col, piece) * rows, rows)
                right[piece * rows:(piece + 1) * rows, :] = right_all[pl.ds(start, rows), :]
            for earlier in range(slot):
                add_block(earlier, 1)
        pass_on(slot, 1)
        make_factors(slot)
        add_block(slot, 0)
        if slot >= half:
            add_block(slot, 1)
    if aligned:
        sides = side[...].astype(jnp.bfloat16)
    else:
        for block in range(nband):
            part = side[:, block * width:(block + 1) * width]
            side_parts[block] = part.astype(jnp.bfloat16)
        sides = jnp.concatenate([side_parts[flip(me, 2 * k)] for k in range(half)], axis=1)

    across = {}
    group = max(1, ncol // 2)
    for low in range(ncol - group, -1, -group):
        product = jnp.dot(
            right[low * rows:(low + group) * rows, :], sides, preferred_element_type=jnp.float32
        )
        own[low * rows:(low + group) * rows, :] = product[:, 0:width]
        for piece in range(low + group - 1, low - 1, -1):
            at = slice((piece - low) * rows, (piece - low + 1) * rows)
            for k in range(half - 1, 0, -1):
                band_out[piece, k] = product[at, k * width:(k + 1) * width].astype(jnp.bfloat16)
                across[piece, k] = pltpu.make_async_remote_copy(
                    src_ref=band_out.at[piece, k],
                    dst_ref=band_in.at[piece, k],
                    send_sem=band_send.at[piece, k],
                    recv_sem=band_recv.at[piece, k],
                    device_id=(flip(me, 2 * k), col),
                    device_id_type=MESH,
                )
                across[piece, k].start()

    last = {}
    for piece in range(ncol - 1, -1, -1):
        value = own[piece * rows:(piece + 1) * rows, :]
        for k in range(1, half):
            across[piece, k].wait_recv()
            value = value + band_in[piece, k].astype(jnp.float32)
        if piece == 0:
            break
        col_out[piece] = value.astype(jnp.bfloat16)
        last[piece] = pltpu.make_async_remote_copy(
            src_ref=col_out.at[piece],
            dst_ref=col_in.at[piece],
            send_sem=col_send.at[piece],
            recv_sem=col_recv.at[piece],
            device_id=(me, flip(col, piece)),
            device_id_type=MESH,
        )
        last[piece].start()
    for piece in range(1, ncol):
        last[piece].wait_recv()
        value = value + col_in[piece].astype(jnp.float32)
    out_ref[...] = value * scale

    for group_of in (arriving, swap, across, last):
        for copy in group_of.values():
            copy.wait_send()


def local(nband, ncol, intersections, screened, poles, gap_energy, gap_class):
    bands, g_rows, states = intersections.shape
    depth, columns = screened.shape
    classes = gap_energy.shape[0]
    half, width, rows = nband // 2, states // nband, states // ncol
    scale = 1.0 / math.sqrt(columns * ncol * bands * nband)
    bf16, f32 = jnp.bfloat16, jnp.float32
    dma = pltpu.SemaphoreType.DMA
    aligned = width % 128 == 0
    lanes = half * width if aligned else states
    shares = 1 + 2 * (half if aligned else 1)
    block = pl.pallas_call(
        functools.partial(kernel, nband, ncol, classes, scale, aligned),
        out_shape=jax.ShapeDtypeStruct((rows, width), f32),
        in_specs=[pl.BlockSpec(memory_space=pl.ANY)] * 5,
        out_specs=pl.BlockSpec(memory_space=pltpu.VMEM),
        scratch_shapes=[
            pltpu.VMEM((2, bands, g_rows, lanes), bf16),
            pltpu.VMEM((nband, 2, depth, columns), bf16),
            pltpu.SMEM((classes,), f32),
            pltpu.VMEM((2, bands, lanes), jnp.int32),
            pltpu.VMEM((2, bands, columns, states), bf16),
            pltpu.VMEM((nband, classes * columns, depth), bf16),
            pltpu.VMEM((2 * bands * columns, lanes), f32),
            pltpu.VMEM((1 if aligned else nband, 2 * bands * columns, width), bf16),
            pltpu.VMEM((states, 2 * bands * columns), bf16),
            pltpu.VMEM((states, 2 * bands * columns), bf16),
            pltpu.VMEM((states, width), f32),
            pltpu.VMEM((ncol, half, rows, width), bf16),
            pltpu.VMEM((ncol, half, rows, width), bf16),
            pltpu.VMEM((ncol, rows, width), bf16),
            pltpu.VMEM((ncol, rows, width), bf16),
            dma((3 + shares,)),
            dma((nband, 2)), dma((nband, 2)),
            dma((shares,)), dma((shares,)),
            dma((ncol, half)), dma((ncol, half)),
            dma((ncol,)), dma((ncol,)),
        ],
        compiler_params=pltpu.CompilerParams(
            collective_id=0, has_side_effects=True, vmem_limit_bytes=56 * 1024 * 1024
        ),
        name="self_energy",
    )(intersections, screened, poles, gap_energy, gap_class)
    return block.T


def solution(mesh):
    return jax.shard_map(
        functools.partial(local, mesh.shape["band"], mesh.shape["col"]),
        mesh=mesh,
        in_specs=(P("band", None, None), P("band", "col"), P("band", "col"), P(), P("band", None)),
        out_specs=P("band", "col"),
        check_vma=False,
    )
```

```python
import functools
import math

import jax
import jax.numpy as jnp
from jax import lax
from jax.experimental import pallas as pl
from jax.experimental.pallas import tpu as pltpu
from jax.sharding import PartitionSpec as P

MESH = pl.DeviceIdType.MESH


def flip(pos, mask):
    bit = 1
    while bit <= mask:
        if mask & bit:
            pos = pos + bit - 2 * bit * lax.rem(lax.div(pos, bit), 2)
        bit *= 2
    return pos


def kernel(
    nband, ncol, classes, scale, aligned,
    inter_ref, screened_ref, poles_ref, energy_ref, class_ref, out_ref,
    inter, held, energies, cls, cross, factors, side, side_parts, right_all, right, own,
    band_out, band_in, col_out, col_in,
    load_sem, gather_send, gather_recv, swap_send, swap_recv,
    band_send, band_recv, col_send, col_recv,
):
    me, col = lax.axis_index("band"), lax.axis_index("col")
    bands, _, states = inter_ref.shape
    depth, columns = screened_ref.shape
    half = nband // 2
    width = states // nband
    rows = states // ncol
    sibling = flip(me, 1)
    first = pl.multiple_of(col * columns, columns)

    barrier = pltpu.get_barrier_semaphore()
    peers = [(flip(me, mask), col) for mask in list(range(2, nband, 2)) + [1]]
    peers += [(me, flip(col, piece)) for piece in range(1, ncol)]
    for peer in peers:
        pl.semaphore_signal(barrier, inc=1, device_id=peer, device_id_type=MESH)

    def shares(owner, slot):
        out = [(inter_ref.at[:, pl.ds(first, columns), :], cross.at[slot])]
        if not aligned:
            out += [(class_ref, cls.at[slot]), (inter_ref, inter.at[slot])]
            return out
        for k in range(half):
            start = pl.multiple_of(flip(owner, 2 * k) * width, width)
            lanes = slice(k * width, (k + 1) * width)
            out.append((class_ref.at[:, pl.ds(start, width)], cls.at[slot, :, lanes]))
            out.append((inter_ref.at[:, :, pl.ds(start, width)], inter.at[slot, :, :, lanes]))
        return out

    pairs = [
        (screened_ref, held.at[0, 0]), (poles_ref, held.at[0, 1]), (energy_ref, energies),
    ] + shares(me, 0)
    loads = [
        pltpu.make_async_copy(source, target, load_sem.at[n])
        for n, (source, target) in enumerate(pairs)
    ]
    pl.semaphore_wait(barrier, len(peers))

    arriving = {}

    def push(slot, bit, part):
        source = (screened_ref, poles_ref)[part] if slot == 0 else held.at[slot, part]
        copy = pltpu.make_async_remote_copy(
            src_ref=source,
            dst_ref=held.at[slot + bit, part],
            send_sem=gather_send.at[slot + bit, part],
            recv_sem=gather_recv.at[slot + bit, part],
            device_id=(flip(me, bit), col),
            device_id_type=MESH,
        )
        copy.start()
        arriving[slot + bit, part] = copy

    bit = half
    while bit:
        push(0, bit, 0)
        push(0, bit, 1)
        bit //= 2
    swap = {}
    for n, (source, target) in enumerate(shares(sibling, 1)):
        swap[n] = pltpu.make_async_remote_copy(
            src_ref=source,
            dst_ref=target,
            send_sem=swap_send.at[n],
            recv_sem=swap_recv.at[n],
            device_id=(sibling, col),
            device_id_type=MESH,
        )
        swap[n].start()
    for load in loads:
        load.start()
    for load in loads:
        load.wait()

    def make_factors(slot):
        amps = held[slot, 0].astype(jnp.float32).T
        freqs = held[slot, 1].astype(jnp.float32).T
        top, square = amps * freqs, freqs * freqs
        for class_id in range(classes):
            energy = energies[class_id]
            factor = (top / (square + energy * energy)).astype(jnp.bfloat16)
            factors[slot, class_id * columns:(class_id + 1) * columns, :] = factor

    def add_block(slot, core):
        start = pl.multiple_of(flip(me, slot) * depth, depth)
        for index in range(bands):
            terms = jnp.dot(
                factors[slot], inter[core, index, pl.ds(start, depth), :],
                preferred_element_type=jnp.float32,
            )
            picked = jnp.zeros((columns, terms.shape[1]), jnp.float32)
            for class_id in range(classes):
                term = terms[class_id * columns:(class_id + 1) * columns]
                picked = jnp.where(cls[core, index:index + 1, :] == class_id, term, picked)
            low = (core * bands + index) * columns
            place = slice(low, low + columns)
            side[place, :] = picked if slot == 0 else side[place, :] + picked

    def turn(core):
        for band in range(bands):
            block = cross[core, band].astype(jnp.float32)
            low = (core * bands + band) * columns
            right_all[:, low:low + columns] = block.T.astype(jnp.bfloat16)

    make_factors(0)
    add_block(0, 0)
    turn(0)

    def pass_on(slot, part):
        arriving[slot, part].wait_recv()
        bit = (slot & -slot) // 2
        while bit:
            push(slot, bit, part)
            bit //= 2

    for slot in range(1, nband):
        pass_on(slot, 0)
        if slot == half:
            for copy in swap.values():
                copy.wait_recv()
            turn(1)
            for piece in range(ncol):
                start = pl.multiple_of(flip(col, piece) * rows, rows)
                right[piece * rows:(piece + 1) * rows, :] = right_all[pl.ds(start, rows), :]
            for earlier in range(slot):
                add_block(earlier, 1)
        pass_on(slot, 1)
        make_factors(slot)
        add_block(slot, 0)
        if slot >= half:
            add_block(slot, 1)
    if aligned:
        sides = side[...].astype(jnp.bfloat16)
    else:
        for block in range(nband):
            part = side[:, block * width:(block + 1) * width]
            side_parts[block] = part.astype(jnp.bfloat16)
        sides = jnp.concatenate([side_parts[flip(me, 2 * k)] for k in range(half)], axis=1)

    across = {}
    group = max(1, ncol // 2)
    for low in range(ncol - group, -1, -group):
        product = jnp.dot(
            right[low * rows:(low + group) * rows, :], sides, preferred_element_type=jnp.float32
        )
        own[low * rows:(low + group) * rows, :] = product[:, 0:width]
        for piece in range(low + group - 1, low - 1, -1):
            at = slice((piece - low) * rows, (piece - low + 1) * rows)
            for k in range(half - 1, 0, -1):
                band_out[piece, k] = product[at, k * width:(k + 1) * width].astype(jnp.bfloat16)
                across[piece, k] = pltpu.make_async_remote_copy(
                    src_ref=band_out.at[piece, k],
                    dst_ref=band_in.at[piece, k],
                    send_sem=band_send.at[piece, k],
                    recv_sem=band_recv.at[piece, k],
                    device_id=(flip(me, 2 * k), col),
                    device_id_type=MESH,
                )
                across[piece, k].start()

    last = {}
    for piece in range(ncol - 1, -1, -1):
        value = own[piece * rows:(piece + 1) * rows, :]
        for k in range(1, half):
            across[piece, k].wait_recv()
            value = value + band_in[piece, k].astype(jnp.float32)
        if piece == 0:
            break
        col_out[piece] = value.astype(jnp.bfloat16)
        last[piece] = pltpu.make_async_remote_copy(
            src_ref=col_out.at[piece],
            dst_ref=col_in.at[piece],
            send_sem=col_send.at[piece],
            recv_sem=col_recv.at[piece],
            device_id=(me, flip(col, piece)),
            device_id_type=MESH,
        )
        last[piece].start()
    for piece in range(1, ncol):
        last[piece].wait_recv()
        value = value + col_in[piece].astype(jnp.float32)
    out_ref[...] = value * scale

    for group_of in (arriving, swap, across, last):
        for copy in group_of.values():
            copy.wait_send()


def local(nband, ncol, intersections, screened, poles, gap_energy, gap_class):
    bands, g_rows, states = intersections.shape
    depth, columns = screened.shape
    classes = gap_energy.shape[0]
    half, width, rows = nband // 2, states // nband, states // ncol
    scale = 1.0 / math.sqrt(columns * ncol * bands * nband)
    bf16, f32 = jnp.bfloat16, jnp.float32
    dma = pltpu.SemaphoreType.DMA
    aligned = width % 128 == 0
    lanes = half * width if aligned else states
    shares = 1 + 2 * (half if aligned else 1)
    block = pl.pallas_call(
        functools.partial(kernel, nband, ncol, classes, scale, aligned),
        out_shape=jax.ShapeDtypeStruct((rows, width), f32),
        in_specs=[pl.BlockSpec(memory_space=pl.ANY)] * 5,
        out_specs=pl.BlockSpec(memory_space=pltpu.VMEM),
        scratch_shapes=[
            pltpu.VMEM((2, bands, g_rows, lanes), bf16),
            pltpu.VMEM((nband, 2, depth, columns), bf16),
            pltpu.SMEM((classes,), f32),
            pltpu.VMEM((2, bands, lanes), jnp.int32),
            pltpu.VMEM((2, bands, columns, states), bf16),
            pltpu.VMEM((nband, classes * columns, depth), bf16),
            pltpu.VMEM((2 * bands * columns, lanes), f32),
            pltpu.VMEM((1 if aligned else nband, 2 * bands * columns, width), bf16),
            pltpu.VMEM((states, 2 * bands * columns), bf16),
            pltpu.VMEM((states, 2 * bands * columns), bf16),
            pltpu.VMEM((states, width), f32),
            pltpu.VMEM((ncol, half, rows, width), bf16),
            pltpu.VMEM((ncol, half, rows, width), bf16),
            pltpu.VMEM((ncol, rows, width), bf16),
            pltpu.VMEM((ncol, rows, width), bf16),
            dma((3 + shares,)),
            dma((nband, 2)), dma((nband, 2)),
            dma((shares,)), dma((shares,)),
            dma((ncol, half)), dma((ncol, half)),
            dma((ncol,)), dma((ncol,)),
        ],
        compiler_params=pltpu.CompilerParams(
            collective_id=0, has_side_effects=True, vmem_limit_bytes=56 * 1024 * 1024
        ),
        name="self_energy",
    )(intersections, screened, poles, gap_energy, gap_class)
    return block.T


def solution(mesh):
    return jax.shard_map(
        functools.partial(local, mesh.shape["band"], mesh.shape["col"]),
        mesh=mesh,
        in_specs=(P("band", None, None), P("band", "col"), P("band", "col"), P(), P("band", None)),
        out_specs=P("band", "col"),
        check_vma=False,
    )
```
